32 devices in a mesh: grp: 2 (over x), len: 16 (over z, y, core).
Axes of the slice: x: 2, y: 2, z: 4, core: 2. Of those that a mesh axis runs over, the one named last changes fastest.
Arguments:
- tin_temp: float32 [64, 512, 1024], P(None, ('grp', 'len')), parts along dimension 1, may hold values from -6 to 6
- flow_code: int32 [64, 512, 1024], P(None, ('grp', 'len')), parts along dimension 1, may hold values from 0 to 3
- speeds: float32 [2, 64], replicated, may hold values from 0.02 to 0.12
- floor_temp: float32 [32, 48, 64, 256], P(('grp', 'len')), parts along dimension 0, may hold values from -6 to 6
- material: int32 [32, 48, 64, 256], P(('grp', 'len')), parts along dimension 0, may hold values from 0 to 2
- conductivity: float32 [3], replicated, may hold values from 0.03 to 0.15
Outputs:
- tin_out: float32 [64, 512, 1024], P(None, ('grp', 'len')), parts along dimension 1
- floor_out: float32 [32, 48, 64, 256], P(('grp', 'len')), parts along dimension 0
The draws below stay inside these ranges and needn't reach their ends.
There are 2 independent parts, one for each index of `grp`. The reference program is written for one: setup_inputs(seed, part) draws one part's arguments, and reference() takes and returns one part's arrays. A program takes and returns all parts, laid end to end along the dimension named above; an argument that names none is the same for every part. Nothing has to cross between parts.
Inputs may be any that keep to these rules, and one draw needn't show every extreme that they name: flow_code % 2 is 0 where the tin cell takes its length upwind value from the lower length index and 1 from the higher; flow_code // 2 likewise across the width. material ids index conductivity.
All inputs are finite; a program needn't handle non-finite values.
Results may differ from the reference program's by a relative error of at most 0.0003.
Values sent between devices are 32-bit elements; how exact they have to be, the bound alone decides.
A program may use at most 128 MiB of HBM per device.

```python
import jax
import jax.numpy as jnp

NY = 1024
ZT = 64
ZR = 48
TILE_Y = 4
MATS = 3
SWEEPS = 2
NX = 256
TILE_X = 4
CXR = 64
CYR = 256
N_LEN = 16


def plant(drawn, own_key, least, high):
    place = [jax.random.randint(jax.random.fold_in(own_key, axis), (), 0, length) for axis, length in enumerate(drawn.shape)]
    longest = drawn.shape.index(max(drawn.shape))
    neighbour = place[:longest] + [(place[longest] + 1) % drawn.shape[longest]] + place[longest + 1:]
    return drawn.at[tuple(place)].set(least).at[tuple(neighbour)].set(high)


def levels(rng, dims, cuts, least, top_value):
    factor_of = 1.0
    for axis_at, blocks in cuts:
        draws = jax.random.uniform(jax.random.fold_in(jax.random.fold_in(rng, 6), axis_at), (blocks,), jnp.float32, least / len(cuts), top_value / len(cuts))
        factor_of = factor_of * jnp.repeat(jnp.exp(draws), dims[axis_at] // blocks).reshape((-1,) + (1,) * (len(dims) - 1 - axis_at))
    return factor_of


def scatter_about(own_key, shape, deviation, limit, cuts=(), dtype=jnp.bfloat16):
    values = deviation * jax.random.normal(own_key, shape, jnp.float32)
    if cuts:
        values = values * levels(own_key, shape, cuts, -0.22, 0.18)
    return jnp.clip(values, -limit, limit).astype(dtype)


def setup_inputs(seed: int = 0, part: int = 0) -> dict:
    seeds = jax.random.split(jax.random.key(seed), 7)
    part_keys = jax.random.split(jax.random.fold_in(seeds[6], part), 7)
    tin_temp = scatter_about(part_keys[0], (ZT, NX, NY), 1.0, 6.0, ((1, 16),), jnp.float32)
    flow_code = plant(jax.random.randint(part_keys[1], (ZT, NX, NY), 0, 4), jax.random.fold_in(part_keys[1], 1), 0, 3).astype(jnp.int32)
    speeds = jnp.clip(jax.random.uniform(seeds[2], (2, ZT), jnp.float32, 0.02, 0.12), 0.02, 0.12)
    floor_temp = scatter_about(part_keys[3], (N_LEN, ZR, CXR, CYR), 1.0, 6.0, ((0, 16),), jnp.float32)
    material = plant(jax.random.randint(part_keys[4], (N_LEN, ZR, CXR, CYR), 0, MATS), jax.random.fold_in(part_keys[4], 1), 0, MATS - 1).astype(jnp.int32)
    conductivity = jnp.clip(jax.random.uniform(seeds[5], (MATS,), jnp.float32, 0.03, 0.15), 0.03, 0.15)
    return {"tin_temp": tin_temp, "flow_code": flow_code, "speeds": speeds, "floor_temp": floor_temp, "material": material, "conductivity": conductivity}


KT = 0.1
HT = 0.2
HR = 0.2


def lookup(material, conductivity):
    result = jnp.zeros(material.shape, jnp.float32)
    for material_id in range(conductivity.shape[0]):
        result = result + jnp.where(material == material_id, conductivity[material_id], 0.0)
    return result


def tin_update(tin_field, padded, flow_code, speeds, top_plane):
    x_minus = padded[:, :-2, 1:-1]
    x_plus = padded[:, 2:, 1:-1]
    y_minus = padded[:, 1:-1, :-2]
    y_plus = padded[:, 1:-1, 2:]
    layer_above = jnp.concatenate([tin_field[1:], tin_field[-1:]], 0)
    layer_below = jnp.concatenate([tin_field[:1], tin_field[:-1]], 0)
    spread = x_minus + x_plus + y_minus + y_plus + layer_above + layer_below - 6.0 * tin_field
    speed_x = speeds[0][:, None, None]
    speed_y = speeds[1][:, None, None]
    carried = jnp.where(flow_code % 2 == 0, speed_x * (x_minus - tin_field), speed_x * (x_plus - tin_field))
    carried = carried + jnp.where(flow_code // 2 == 0, speed_y * (y_minus - tin_field), speed_y * (y_plus - tin_field))
    layer_ids = jnp.arange(tin_field.shape[0])[:, None, None]
    contact = jnp.where(layer_ids == 0, HT * (top_plane[None] - tin_field[0:1]), 0.0)
    return tin_field + KT * spread + carried + contact


def floor_update(floor_field, conduct, along_x, conduct_x, along_y, conduct_y, bottom_tin):
    lateral = 0.5 * (conduct + conduct_x[:, :-2]) * (along_x[:, :-2] - floor_field)
    lateral = lateral + 0.5 * (conduct + conduct_x[:, 2:]) * (along_x[:, 2:] - floor_field)
    lateral = lateral + 0.5 * (conduct + conduct_y[:, :, :-2]) * (along_y[:, :, :-2] - floor_field)
    lateral = lateral + 0.5 * (conduct + conduct_y[:, :, 2:]) * (along_y[:, :, 2:] - floor_field)
    field_above = jnp.concatenate([floor_field[:1], floor_field[:-1]], 0)
    conduct_above = jnp.concatenate([conduct[:1], conduct[:-1]], 0)
    field_below = jnp.concatenate([floor_field[1:], jnp.zeros_like(floor_field[:1])], 0)
    conduct_below = jnp.concatenate([conduct[1:], jnp.zeros_like(conduct[:1])], 0)
    vertical = 0.5 * (conduct + conduct_above) * (field_above - floor_field)
    vertical = vertical + 0.5 * (conduct + conduct_below) * (field_below - floor_field)
    layer_ids = jnp.arange(floor_field.shape[0])[:, None, None]
    contact = jnp.where(layer_ids == 0, HR * (bottom_tin[None] - floor_field[0:1]), 0.0)
    return floor_field + lateral + vertical + contact


def to_grid(tile_array):
    shaped = tile_array.reshape(TILE_X, TILE_Y, ZR, CXR, CYR)
    return shaped.transpose(2, 0, 3, 1, 4).reshape(ZR, NX, NY)


def to_tiles(grid_array):
    shaped = grid_array.reshape(ZR, TILE_X, CXR, TILE_Y, CYR)
    return shaped.transpose(1, 3, 0, 2, 4).reshape(N_LEN, ZR, CXR, CYR)


def reference(tin_temp, flow_code, speeds, floor_temp, material, conductivity):
    tin_field = tin_temp
    floor_field = to_grid(floor_temp)
    conduct = lookup(to_grid(material), conductivity)
    pad_x = ((0, 0), (1, 1), (0, 0))
    pad_y = ((0, 0), (0, 0), (1, 1))
    conduct_x = jnp.pad(conduct, pad_x)
    conduct_y = jnp.pad(conduct, pad_y)
    for repeat in range(SWEEPS):
        bottom_tin = tin_field[0]
        top_plane = floor_field[0]
        padded = jnp.pad(tin_field, ((0, 0), (1, 1), (1, 1)))
        tin_next = tin_update(tin_field, padded, flow_code, speeds, top_plane)
        floor_next = floor_update(floor_field, conduct, jnp.pad(floor_field, pad_x), conduct_x,
                                  jnp.pad(floor_field, pad_y), conduct_y, bottom_tin)
        tin_field = tin_next
        floor_field = floor_next
    return tin_field, to_tiles(floor_field)
```

```python
import functools

import jax
import jax.numpy as jnp
from jax import lax
from jax.experimental import pallas as pl
from jax.experimental.pallas import tpu as pltpu
from jax.sharding import PartitionSpec as P

KT = 0.1
HT = 0.2
HR = 0.2
L = 128
S = 8
NQ = 4
FQ = 2
TU = 2
FU = 1
PU = 2


def kernel(n, ty, tin_h, flow_h, speeds_h, floor_h, mat_h, cond_h,
           tin_o, floor_o,
           speeds, cond, tin0, flow, tin1, floor0, mat, floor1, kh, kx, ky, kz, pz,
           cs, cl, cr, kd, fd, pp, bb, load_sem, send_sem, recv_sem):
    Z, R, NYW = tin_h.shape
    ZF, CX, CY = floor_h.shape
    NH, NK = R // S, NYW // L
    NI, NJ = CX // S, CY // L
    ZQ, ZC = Z // NQ, ZF // FQ
    me = lax.axis_index("len")
    c = lax.rem(me, ty)
    base = me - c
    up_ok, dn_ok = me < n - 1, me > 0
    rup_ok, rdn_ok = me + ty < n, me >= ty
    cup_ok, cdn_ok = c < ty - 1, c > 0

    numbers = iter(range(10 ** 6))

    def local_copy(src, dst):
        return pltpu.make_async_copy(src, dst, load_sem.at[next(numbers)])

    get_cond, get_speeds = local_copy(cond_h, cond), local_copy(speeds_h, speeds)
    get_floor = []
    for q in range(FQ):
        part = pl.ds(q * ZC, ZC)
        get_floor.append(
            [local_copy(mat_h.at[part, :, pl.ds(j * L, L)], mat.at[part, j, pl.ds(S, CX), :]) for j in range(NJ)]
            + [local_copy(floor_h.at[part, :, pl.ds(j * L, L)], floor0.at[part, j, pl.ds(S, CX), :])
               for j in range(NJ)])
    get_tin = []
    for q in range(NQ):
        part = pl.ds(q * ZQ, ZQ)
        get_tin.append(
            [local_copy(tin_h.at[part, :, pl.ds(k * L, L)], tin0.at[pl.ds(q * ZQ + 1, ZQ), k, pl.ds(S, R), :])
             for k in range(NK)] + [local_copy(flow_h.at[part], flow.at[part])])
    get_cond.start()
    get_speeds.start()

    barrier = pltpu.get_barrier_semaphore()

    def hello(target):
        pl.semaphore_signal(barrier, inc=1, device_id={"len": target},
                            device_id_type=pl.DeviceIdType.MESH)

    for d in range(1, ty):
        hello(base + lax.rem(c + d, ty))
    pairs = [(rup_ok, me + ty), (rdn_ok, me - ty),
             (jnp.logical_and(c == ty - 1, up_ok), me + 1),
             (jnp.logical_and(c == 0, dn_ok), me - 1)]
    for ok, target in pairs:
        @pl.when(ok)
        def _():
            hello(target)

    for group in get_floor + get_tin:
        for ld in group:
            ld.start()

    row = lax.broadcasted_iota(jnp.int32, (S, L), 0)
    lane = lax.broadcasted_iota(jnp.int32, (S, L), 1)
    row_first = row == 0
    lane_first, lane_last = lane == 0, lane == L - 1
    lane_even = (lane & 1) == 0
    zero = jnp.zeros((S, L), jnp.float32)

    links = iter(range(10 ** 6))

    def remote(src, dst, target):
        e = next(links)
        return pltpu.make_async_remote_copy(
            src_ref=src, dst_ref=dst, send_sem=send_sem.at[e],
            recv_sem=recv_sem.at[e], device_id={"len": target},
            device_id_type=pl.DeviceIdType.MESH)

    def both_ways(up, down, ok_up, ok_dn):
        return [(ok_up, ok_dn, up), (ok_dn, ok_up, down)]

    lo, hi = S - 1, S + R
    flo, fhi = S - 1, S + CX
    planes = pl.ds(1, Z)
    t0 = both_ways(
        [remote(tin_h.at[:, R - 1, pl.ds(k * L, L)], tin0.at[planes, k, lo, :], me + 1) for k in range(NK)],
        [remote(tin_h.at[:, 0, pl.ds(k * L, L)], tin0.at[planes, k, hi, :], me - 1) for k in range(NK)],
        up_ok, dn_ok)
    layers = pl.ds(0, ZF)
    r0 = both_ways(
        [remote(a.at[:, CX - 1, pl.ds(j * L, L)], b.at[layers, j, flo, :], me + ty)
         for a, b in ((floor_h, floor0), (mat_h, mat)) for j in range(NJ)],
        [remote(a.at[:, 0, pl.ds(j * L, L)], b.at[layers, j, fhi, :], me - ty)
         for a, b in ((floor_h, floor0), (mat_h, mat)) for j in range(NJ)],
        rup_ok, rdn_ok)
    c0 = both_ways([remote(cs.at[0:2], cl.at[0:2], me + 1)], [remote(cs.at[0:2], cr.at[0:2], me - 1)],
                   cup_ok, cdn_ok)
    t1 = both_ways([remote(tin1.at[planes, :, S + R - 1, :], tin1.at[planes, :, lo, :], me + 1)],
                   [remote(tin1.at[planes, :, S, :], tin1.at[planes, :, hi, :], me - 1)],
                   up_ok, dn_ok)
    r1 = both_ways([remote(floor1.at[layers, :, S + CX - 1, :], floor1.at[layers, :, flo, :], me + ty)],
                   [remote(floor1.at[layers, :, S, :], floor1.at[layers, :, fhi, :], me - ty)],
                   rup_ok, rdn_ok)
    c1 = both_ways([remote(cs.at[2], cl.at[2], me + 1)], [remote(cs.at[2], cr.at[2], me - 1)],
                   cup_ok, cdn_ok)

    def floor_part(field, t):
        return field.at[0, :, pl.ds(pl.multiple_of(S + t * R, S), R), :]

    def tin_part(field, t):
        return field.at[1, pl.ds(NJ * t, NJ), pl.ds(S, R), :]

    def p_into(e):
        return pp.at[e, pl.ds(NJ * c, NJ), :, :]

    def b_into(e):
        return bb.at[e, :, pl.ds(pl.multiple_of(c * R, S), R), :]

    def to_group(part, into):
        out = []
        for d in range(1, ty):
            t = lax.rem(c + d, ty)
            out.append(remote(part(t), into, base + t))
        return out

    p0 = to_group(functools.partial(floor_part, floor0), p_into(0))
    b0 = to_group(functools.partial(tin_part, tin0), b_into(0))
    p1 = to_group(functools.partial(floor_part, floor1), p_into(1))
    b1 = to_group(functools.partial(tin_part, tin1), b_into(1))
    own_p0, own_p1 = local_copy(floor_part(floor0, c), p_into(0)), local_copy(floor_part(floor1, c), p_into(1))
    own_b0, own_b1 = local_copy(tin_part(tin0, c), b_into(0)), local_copy(tin_part(tin1, c), b_into(1))

    def start_if(msgs):
        for ok, _, copies in msgs:
            @pl.when(ok)
            def _():
                for m in copies:
                    m.start()

    def wait_recv_if(msgs):
        for _, ok, copies in msgs:
            @pl.when(ok)
            def _():
                for m in copies:
                    m.wait_recv()

    def wait_send_if(msgs):
        for ok, _, copies in msgs:
            @pl.when(ok)
            def _():
                for m in copies:
                    m.wait_send()

    def clear(ok, fields, first):
        @pl.when(jnp.logical_not(ok))
        def _():
            for ref in fields:
                def body(z, carry):
                    for k in range(ref.shape[1]):
                        ref[z, k, pl.ds(first, S), :] = zero
                    return carry

                lax.fori_loop(0, ref.shape[0], body, 0)

    clear(dn_ok, (tin0, tin1), 0)
    clear(up_ok, (tin0, tin1), S + R)
    clear(rdn_ok, (floor0, floor1), 0)
    clear(rup_ok, (floor0, floor1), S + CX)
    for ok, ref in ((cdn_ok, cl), (cup_ok, cr)):
        @pl.when(jnp.logical_not(ok))
        def _():
            ref[...] = jnp.zeros_like(ref)
    cs[...] = jnp.zeros_like(cs)
    for ref in (floor0, floor1, kh):
        for j in range(NJ):
            for i in range(NI):
                ref[ZF, j, pl.ds(S + i * S, S), :] = zero

    peers = ty - 1
    for ok, _ in pairs:
        peers = peers + ok.astype(jnp.int32)
    pl.semaphore_wait(barrier, peers)
    start_if(r0)
    start_if(t0)

    get_cond.wait()
    k0, k1, k2 = cond[0] * 0.5, cond[1] * 0.5, cond[2] * 0.5

    def lookup(m):
        return jnp.where(m == 0, k0, jnp.where(m == 1, k1, k2))

    def pack_columns(slot, z, i, first, last):
        mine = lax.shift_right_logical(lane, 1) == z
        both = pltpu.roll(jnp.where(lane_last, last, first), 2 * z + 1, 1)
        pltpu.store(cs.at[slot, pl.ds(i * S, S), :], both, mask=mine)

    def prepare(z, carry):
        for i in range(NI):
            at = pl.ds(S + i * S, S)
            k = [lookup(mat[z, j, at, :]) for j in range(NJ)]
            for j in range(NJ):
                kh[z, j, at, :] = k[j]
            pack_columns(0, z, i, k[0], k[NJ - 1])
            pack_columns(1, z, i, floor0[z, 0, at, :], floor0[z, NJ - 1, at, :])
        return carry

    for q in range(FQ):
        for ld in get_floor[q]:
            ld.wait()
        lax.fori_loop(q * ZC, (q + 1) * ZC, prepare, 0, unroll=PU)
    start_if(c0)
    for m in p0:
        m.start()
    own_p0.start()

    def tin_ghosts(e, src):
        for k in range(NK):
            for h in range(NH):
                at = pl.ds(S + h * S, S)
                u = src[1, k, at, :]
                src[0, k, at, :] = u + (HT / KT) * (pp[e, k, pl.ds(h * S, S), :] - u)

    def tin_copy_last(src):
        for k in range(NK):
            src[Z + 1, k, pl.ds(S, R), :] = src[Z, k, pl.ds(S, R), :]

    def tin_layer(src, put, z):
        s_x, s_y = speeds[0, z], speeds[1, z]
        keep = (1.0 - 6.0 * KT) - s_x - s_y

        def at(p, h, k, shift=0):
            return src[p, k, pl.ds(S + h * S + shift, S), :]

        u = functools.cache(lambda h, k: at(z + 1, h, k))
        ld = functools.cache(lambda h, k: pltpu.roll(u(h, k), 1, 1))
        lu = functools.cache(lambda h, k: pltpu.roll(u(h, k), L - 1, 1))
        for k in range(NK):
            for h in range(NH):
                xm, xp = at(z + 1, h, k, -1), at(z + 1, h, k, 1)
                ym = jnp.where(lane_first, 0.0 if k == 0 else ld(h, k - 1), ld(h, k))
                yp = jnp.where(lane_last, 0.0 if k == NK - 1 else lu(h, k + 1), lu(h, k))
                f = flow[z, pl.ds(h * S, S), pl.ds(k * L, L)]
                total = ((xm + xp) + (ym + yp)) + (at(z, h, k) + at(z + 2, h, k))
                new = keep * u(h, k) + KT * total
                new = new + s_x * jnp.where((f & 1) == 0, xm, xp)
                new = new + s_y * jnp.where(f < 2, ym, yp)
                put(z, h, k, new)

    def put_tin1(z, h, k, v):
        tin1[z + 1, k, pl.ds(S + h * S, S), :] = v

    def put_tin_o(z, h, k, v):
        tin_o[z, pl.ds(h * S, S), pl.ds(k * L, L)] = v

    def tin_range(src, put, first, last):
        def body(z, carry):
            tin_layer(src, put, z)
            return carry

        lax.fori_loop(first, last, body, 0, unroll=TU)

    def edge_flux(slot):
        for i in range(NI):
            at = pl.ds(i * S, S)

            def beside(s):
                return jnp.where(lane_even, pltpu.roll(cr[s, at, :], L - 1, 1), pltpu.roll(cl[s, at, :], 1, 1))

            if slot == 1:
                k = cs[0, at, :] + beside(0)
                kd[at, :] = jnp.where(lane_even, k, -k)
            fd[at, :] = kd[at, :] * (beside(slot) - cs[slot, at, :])

    def contact_flux(e, src):
        for j in range(NJ):
            for i in range(NI):
                at = pl.ds(i * S, S)
                pz[j, at, :] = HR * (src[0, j, pl.ds(S + i * S, S), :] - bb[e, j, at, :])

    def floor_layer(first, src, put, z):
        def at(ref, p, j, i, shift=0):
            return ref[p, j, pl.ds(S + i * S + shift, S), :]

        def face_x(j, i):
            if first:
                v = at(kh, z, j, i) + at(kh, z, j, i, 1)
                kx[z, j, pl.ds(S + i * S, S), :] = v
                return v
            return at(kx, z, j, i)

        def flux_x(j, i):
            return face_x(j, i) * (at(src, z, j, i, 1) - at(src, z, j, i))

        rx = [pltpu.roll(flux_x(j, -1), 1, 0) for j in range(NJ)]
        for i in range(NI):
            own = pl.ds(i * S, S)
            g = [at(src, z, j, i) for j in range(NJ)]
            if first:
                k = [at(kh, z, j, i) for j in range(NJ)]
                kr = [pltpu.roll(v, L - 1, 1) for v in k]
                fy_k = []
                for j in range(NJ):
                    v = k[j] + (kr[j] if j == NJ - 1 else jnp.where(lane_last, kr[j + 1], kr[j]))
                    ky[z, j, own, :] = v
                    fy_k.append(v)
            else:
                fy_k = [ky[z, j, own, :] for j in range(NJ)]
            edge = pltpu.roll(fd[own, :], L - 1 - 2 * z, 1)
            gr = [pltpu.roll(v, L - 1, 1) for v in g]
            fy = []
            for j in range(NJ):
                if j == NJ - 1:
                    fy.append(jnp.where(lane_last, edge, fy_k[j] * (gr[j] - g[j])))
                else:
                    fy.append(fy_k[j] * (jnp.where(lane_last, gr[j + 1], gr[j]) - g[j]))
            fr = [pltpu.roll(v, 1, 1) for v in fy]
            new = []
            for j in range(NJ):
                py = jnp.where(lane_first, fr[j - 1] if j else edge, fr[j])
                fx = flux_x(j, i)
                rolled = pltpu.roll(fx, 1, 0)
                px = jnp.where(row_first, rx[j], rolled)
                rx[j] = rolled
                if first:
                    k_z = k[j] + at(kh, z + 1, j, i)
                    kz[z, j, own, :] = k_z
                else:
                    k_z = kz[z, j, own, :]
                fz = k_z * (at(src, z + 1, j, i) - g[j])
                v = (g[j] + (fz - pz[j, own, :])) + ((fx - px) + (fy[j] - py))
                pz[j, own, :] = fz
                put(z, j, i, v)
                new.append(v)
            if first:
                pack_columns(2, z, i, new[0], new[NJ - 1])

    def put_floor1(z, j, i, v):
        floor1[z, j, pl.ds(S + i * S, S), :] = v

    def put_floor_o(z, j, i, v):
        floor_o[z, pl.ds(i * S, S), pl.ds(j * L, L)] = v

    def floor_sweep(first, src, put):
        def body(z, carry):
            floor_layer(first, src, put, z)
            return carry

        lax.fori_loop(0, ZF, body, 0, unroll=FU)

    get_speeds.wait()
    for ld in get_tin[0]:
        ld.wait()
    for m in b0:
        m.start()
    own_b0.start()
    for m in p0:
        m.wait_recv()
    own_p0.wait()
    tin_ghosts(0, tin0)
    wait_recv_if(t0)
    for q in range(NQ):
        if q < NQ - 1:
            for ld in get_tin[q + 1]:
                ld.wait()
        else:
            tin_copy_last(tin0)
        tin_range(tin0, put_tin1, q * ZQ, (q + 1) * ZQ)
    tin_copy_last(tin1)
    start_if(t1)
    for m in b1:
        m.start()
    own_b1.start()

    wait_recv_if(r0)

    def k_halo(z, carry):
        for j in range(NJ):
            for ok, at in ((rdn_ok, pl.ds(0, S)), (rup_ok, pl.ds(S + CX, S))):
                kh[z, j, at, :] = lookup(mat[z, j, at, :]) * ok.astype(jnp.float32)
        return carry

    lax.fori_loop(0, ZF, k_halo, 0, unroll=4)
    wait_recv_if(c0)
    edge_flux(1)
    for m in b0:
        m.wait_recv()
    own_b0.wait()
    contact_flux(0, floor0)
    floor_sweep(True, floor0, put_floor1)
    start_if(r1)
    start_if(c1)
    for m in p1:
        m.start()
    own_p1.start()

    wait_recv_if(t1)
    for m in p1:
        m.wait_recv()
    own_p1.wait()
    tin_ghosts(1, tin1)
    tin_range(tin1, put_tin_o, 0, Z)

    wait_recv_if(r1)
    wait_recv_if(c1)
    for m in b1:
        m.wait_recv()
    own_b1.wait()
    edge_flux(2)
    contact_flux(1, floor1)
    floor_sweep(False, floor1, put_floor_o)

    for msgs in (t0, r0, c0, t1, r1, c1):
        wait_send_if(msgs)
    for m in p0 + b0 + p1 + b1:
        m.wait_send()


def local(n, ty, tin_temp, flow_code, speeds, floor_temp, material, conductivity):
    tin_shape = tin_temp.shape
    floor_shape = floor_temp.shape[1:]
    Z, R, NYW = tin_shape
    ZF, CX, CY = floor_shape
    NK, NJ = NYW // L, CY // L
    f32, i32 = jnp.float32, jnp.int32
    V = pltpu.VMEM
    tin_v, floor_v = V((Z + 2, NK, R + 2 * S, L), f32), V((ZF + 1, NJ, CX + 2 * S, L), f32)
    n_local = 6 + FQ * 2 * NJ + NQ * (NK + 1)
    n_remote = 2 * NK + 4 * NJ + 8 + 4 * (ty - 1)
    tin_out, floor_out = pl.pallas_call(
        functools.partial(kernel, n, ty),
        out_shape=[V(tin_shape, f32), V(floor_shape, f32)],
        in_specs=[pl.BlockSpec(memory_space=pltpu.HBM)] * 6,
        out_specs=[pl.BlockSpec(memory_space=pltpu.VMEM)] * 2,
        scratch_shapes=[
            pltpu.SMEM(speeds.shape, f32), pltpu.SMEM(conductivity.shape, f32),
            tin_v, V(tin_shape, i32), tin_v, floor_v, V((ZF, NJ, CX + 2 * S, L), i32), floor_v,
            floor_v, V((ZF, NJ, CX + S, L), f32), V((ZF, NJ, CX, L), f32), V((ZF, NJ, CX, L), f32),
            V((NJ, CX, L), f32),
            V((3, CX, L), f32), V((3, CX, L), f32), V((3, CX, L), f32), V((CX, L), f32), V((CX, L), f32),
            V((2, NK, R, L), f32), V((2, NJ, CX, L), f32),
            pltpu.SemaphoreType.DMA((n_local,)),
            pltpu.SemaphoreType.DMA((n_remote,)),
            pltpu.SemaphoreType.DMA((n_remote,)),
        ],
        compiler_params=pltpu.CompilerParams(
            collective_id=0, has_side_effects=True, vmem_limit_bytes=52 * 1024 * 1024),
        cost_estimate=pl.CostEstimate(flops=120_000_000, bytes_accessed=23_000_000, transcendentals=0),
    )(tin_temp, flow_code, pltpu.with_memory_space_constraint(speeds, pltpu.HBM), floor_temp[0],
      material[0], pltpu.with_memory_space_constraint(conductivity, pltpu.HBM))
    return tin_out, floor_out[None]


def solution(mesh):
    n = mesh.shape["len"]
    split = ("grp", "len")
    placed = (P(None, split, None), P(None, split, None), P(),
              P(split, None, None, None), P(split, None, None, None), P())

    def whole(tin_temp, flow_code, speeds, floor_temp, material, conductivity):
        ty = tin_temp.shape[2] // floor_temp.shape[3]
        return jax.shard_map(
            functools.partial(local, n, ty),
            mesh=mesh,
            in_specs=placed,
            out_specs=(P(None, split, None), P(split, None, None, None)),
            check_vma=False,
        )(tin_temp, flow_code, speeds, floor_temp, material, conductivity)

    return whole
```

```python
import functools

import jax
import jax.numpy as jnp
from jax import lax
from jax.experimental import pallas as pl
from jax.experimental.pallas import tpu as pltpu
from jax.sharding import PartitionSpec as P

KT = 0.1
HT = 0.2
HR = 0.2
L = 128
S = 8
NQ = 4
FQ = 2
TU = 8
FU = 8
PU = 8


def kernel(n, ty, tin_h, flow_h, speeds_h, floor_h, mat_h, cond_h,
           tin_o, floor_o,
           speeds, cond, tin0, flow, tin1, floor0, mat, floor1, kh, kx, kyp, kym, kz, pz,
           cs, cl, cr, kd, fd, pp, bb, load_sem, send_sem, recv_sem):
    Z, R, NYW = tin_h.shape
    ZF, CX, CY = floor_h.shape
    NH, NK = R // S, NYW // L
    NI, NJ = CX // S, CY // L
    ZQ, ZC = Z // NQ, ZF // FQ
    me = lax.axis_index("len")
    c = lax.rem(me, ty)
    base = me - c
    up_ok, dn_ok = me < n - 1, me > 0
    rup_ok, rdn_ok = me + ty < n, me >= ty
    cup_ok, cdn_ok = c < ty - 1, c > 0

    numbers = iter(range(10 ** 6))

    def local_copy(src, dst):
        return pltpu.make_async_copy(src, dst, load_sem.at[next(numbers)])

    get_cond, get_speeds = local_copy(cond_h, cond), local_copy(speeds_h, speeds)
    get_floor = []
    for q in range(FQ):
        part = pl.ds(q * ZC, ZC)
        get_floor.append(
            [local_copy(mat_h.at[part, :, pl.ds(j * L, L)], mat.at[part, j, pl.ds(S, CX), :]) for j in range(NJ)]
            + [local_copy(floor_h.at[part, :, pl.ds(j * L, L)], floor0.at[part, j, pl.ds(S, CX), :])
               for j in range(NJ)])
    get_tin = [local_copy(tin_h.at[:, :, pl.ds(k * L, L)], tin0.at[pl.ds(1, Z), k, pl.ds(S, R), :])
               for k in range(NK)] + [local_copy(flow_h, flow)]
    get_cond.start()
    get_speeds.start()

    barrier = pltpu.get_barrier_semaphore()

    def hello(target):
        pl.semaphore_signal(barrier, inc=1, device_id={"len": target},
                            device_id_type=pl.DeviceIdType.MESH)

    for d in range(1, ty):
        hello(base + lax.rem(c + d, ty))
    pairs = [(rup_ok, me + ty), (rdn_ok, me - ty),
             (jnp.logical_and(c == ty - 1, up_ok), me + 1),
             (jnp.logical_and(c == 0, dn_ok), me - 1)]
    for ok, target in pairs:
        @pl.when(ok)
        def _():
            hello(target)

    for group in get_floor:
        for ld in group:
            ld.start()

    row = lax.broadcasted_iota(jnp.int32, (S, L), 0)
    lane = lax.broadcasted_iota(jnp.int32, (S, L), 1)
    row_first = row == 0
    lane_first, lane_last = lane == 0, lane == L - 1
    lane_even = (lane & 1) == 0
    zero = jnp.zeros((S, L), jnp.float32)

    links = iter(range(10 ** 6))

    def remote(src, dst, target):
        e = next(links)
        return pltpu.make_async_remote_copy(
            src_ref=src, dst_ref=dst, send_sem=send_sem.at[e],
            recv_sem=recv_sem.at[e], device_id={"len": target},
            device_id_type=pl.DeviceIdType.MESH)

    def both_ways(up, down, ok_up, ok_dn):
        return [(ok_up, ok_dn, up), (ok_dn, ok_up, down)]

    lo, hi = S - 1, S + R
    flo, fhi = S - 1, S + CX
    planes = pl.ds(1, Z)
    t0 = both_ways(
        [remote(tin_h.at[:, R - 1, pl.ds(k * L, L)], tin0.at[planes, k, lo, :], me + 1) for k in range(NK)],
        [remote(tin_h.at[:, 0, pl.ds(k * L, L)], tin0.at[planes, k, hi, :], me - 1) for k in range(NK)],
        up_ok, dn_ok)
    layers = pl.ds(0, ZF)
    r0 = both_ways(
        [remote(a.at[:, CX - 1, pl.ds(j * L, L)], b.at[layers, j, flo, :], me + ty)
         for a, b in ((floor_h, floor0), (mat_h, mat)) for j in range(NJ)],
        [remote(a.at[:, 0, pl.ds(j * L, L)], b.at[layers, j, fhi, :], me - ty)
         for a, b in ((floor_h, floor0), (mat_h, mat)) for j in range(NJ)],
        rup_ok, rdn_ok)
    c0 = both_ways([remote(cs.at[0:2], cl.at[0:2], me + 1)], [remote(cs.at[0:2], cr.at[0:2], me - 1)],
                   cup_ok, cdn_ok)
    r1 = both_ways([remote(floor1.at[layers, :, S + CX - 1, :], floor1.at[layers, :, flo, :], me + ty)],
                   [remote(floor1.at[layers, :, S, :], floor1.at[layers, :, fhi, :], me - ty)],
                   rup_ok, rdn_ok)
    c1 = both_ways([remote(cs.at[2], cl.at[2], me + 1)], [remote(cs.at[2], cr.at[2], me - 1)],
                   cup_ok, cdn_ok)

    def p_into(e):
        return pp.at[e, pl.ds(NJ * c, NJ), :, :]

    def b_into(e):
        return bb.at[e, :, pl.ds(pl.multiple_of(c * R, S), R), :]

    def p_part(t):
        return floor1.at[0, :, pl.ds(pl.multiple_of(S + t * R, S), R), :]

    def b_part(t):
        return tin1.at[1, pl.ds(NJ * t, NJ), pl.ds(S, R), :]

    def p_parts(t):
        return [(floor_h.at[0, pl.ds(pl.multiple_of(t * R, S), R), pl.ds(j * L, L)], pp.at[0, NJ * c + j])
                for j in range(NJ)]

    def b_parts(t):
        return [(tin_h.at[0, :, pl.ds(pl.multiple_of((NJ * t + j) * L, L), L)],
                 bb.at[0, j, pl.ds(pl.multiple_of(c * R, S), R), :]) for j in range(NJ)]

    group = [lax.rem(c + d, ty) for d in range(1, ty)]
    p0 = [remote(*m, base + t) for t in group for m in p_parts(t)]
    b0 = [remote(*m, base + t) for t in group for m in b_parts(t)]
    p1 = [remote(p_part(t), p_into(1), base + t) for t in group]
    b1 = [remote(b_part(t), b_into(1), base + t) for t in group]
    own0 = [local_copy(*m) for m in p_parts(c) + b_parts(c)]
    own_p1, own_b1 = local_copy(p_part(c), p_into(1)), local_copy(b_part(c), b_into(1))
    t1_first = next(links)

    def t1(q):
        part = pl.ds(q * ZQ + 1, ZQ)

        def one(way, src, dst, target):
            e = t1_first + 2 * q + way
            return pltpu.make_async_remote_copy(
                src_ref=tin1.at[part, :, src, :], dst_ref=tin1.at[part, :, dst, :], send_sem=send_sem.at[e],
                recv_sem=recv_sem.at[e], device_id={"len": target}, device_id_type=pl.DeviceIdType.MESH)

        return both_ways([one(0, S + R - 1, lo, me + 1)], [one(1, S, hi, me - 1)], up_ok, dn_ok)

    def start_if(msgs):
        for ok, _, copies in msgs:
            @pl.when(ok)
            def _():
                for m in copies:
                    m.start()

    def wait_recv_if(msgs):
        for _, ok, copies in msgs:
            @pl.when(ok)
            def _():
                for m in copies:
                    m.wait_recv()

    def wait_send_if(msgs):
        for ok, _, copies in msgs:
            @pl.when(ok)
            def _():
                for m in copies:
                    m.wait_send()

    for m in own0:
        m.start()

    def clear(ok, fields, first):
        @pl.when(jnp.logical_not(ok))
        def _():
            for ref in fields:
                def body(z, carry):
                    for k in range(ref.shape[1]):
                        ref[z, k, pl.ds(first, S), :] = zero
                    return carry

                lax.fori_loop(0, ref.shape[0], body, 0)

    clear(dn_ok, (tin0, tin1), 0)
    clear(up_ok, (tin0, tin1), S + R)
    clear(rdn_ok, (floor0, floor1), 0)
    clear(rup_ok, (floor0, floor1), S + CX)
    for ok, ref in ((cdn_ok, cl), (cup_ok, cr)):
        @pl.when(jnp.logical_not(ok))
        def _():
            ref[...] = jnp.zeros_like(ref)
    cs[...] = jnp.zeros_like(cs)
    for ref in (floor0, floor1, kh):
        for j in range(NJ):
            for i in range(NI):
                ref[ZF, j, pl.ds(S + i * S, S), :] = zero

    peers = ty - 1
    for ok, _ in pairs:
        peers = peers + ok.astype(jnp.int32)
    pl.semaphore_wait(barrier, peers)
    start_if(r0)
    for m in b0 + p0:
        m.start()

    get_cond.wait()
    k0, k1, k2 = cond[0] * 0.5, cond[1] * 0.5, cond[2] * 0.5

    def lookup(m):
        return jnp.where(m == 0, k0, jnp.where(m == 1, k1, k2))

    def pack_columns(slot, z, i, first, last):
        mine = lax.shift_right_logical(lane, 1) == z
        both = pltpu.roll(jnp.where(lane_last, last, first), lax.rem(2 * z + 1 + L, L), 1)
        pltpu.store(cs.at[slot, pl.ds(i * S, S), :], both, mask=mine)

    def prepare(z, carry):
        for i in range(NI):
            at = pl.ds(S + i * S, S)
            k = [lookup(mat[z, j, at, :]) for j in range(NJ)]
            for j in range(NJ):
                kh[z, j, at, :] = k[j]
            pack_columns(0, z, i, k[0], k[NJ - 1])
            pack_columns(1, z, i, floor0[z, 0, at, :], floor0[z, NJ - 1, at, :])
        return carry

    def faces_y(z, carry):
        for i in range(NI):
            own = pl.ds(i * S, S)
            k = [kh[z, j, pl.ds(S + i * S, S), :] for j in range(NJ)]
            after = [pltpu.roll(v, L - 1, 1) for v in k]
            before = [pltpu.roll(v, 1, 1) for v in k]
            for j in range(NJ):
                kyp[z, j, own, :] = k[j] + (
                    after[j] if j == NJ - 1 else jnp.where(lane_last, after[j + 1], after[j]))
                kym[z, j, own, :] = k[j] + (
                    before[j] if j == 0 else jnp.where(lane_first, before[j - 1], before[j]))
        return carry

    for q in range(FQ):
        for ld in get_floor[q]:
            ld.wait()
        if q == FQ - 1:
            for ld in get_tin:
                ld.start()
        lax.fori_loop(q * ZC, (q + 1) * ZC, prepare, 0, unroll=PU)
    start_if(c0)
    start_if(t0)
    lax.fori_loop(0, ZF, faces_y, 0, unroll=PU)

    def tin_ghosts(e, src):
        for k in range(NK):
            for h in range(NH):
                at = pl.ds(S + h * S, S)
                u = src[1, k, at, :]
                src[0, k, at, :] = u + (HT / KT) * (pp[e, k, pl.ds(h * S, S), :] - u)

    def tin_copy_last(src):
        for k in range(NK):
            src[Z + 1, k, pl.ds(S, R), :] = src[Z, k, pl.ds(S, R), :]

    def tin_layer(src, put, z):
        s_x, s_y = speeds[0, z], speeds[1, z]
        keep = (1.0 - 6.0 * KT) - s_x - s_y

        def at(p, h, k, shift=0):
            return src[p, k, pl.ds(S + h * S + shift, S), :]

        u = functools.cache(lambda h, k: at(z + 1, h, k))
        ld = functools.cache(lambda h, k: pltpu.roll(u(h, k), 1, 1))
        lu = functools.cache(lambda h, k: pltpu.roll(u(h, k), L - 1, 1))
        for k in range(NK):
            for h in range(NH):
                xm, xp = at(z + 1, h, k, -1), at(z + 1, h, k, 1)
                ym = jnp.where(lane_first, 0.0 if k == 0 else ld(h, k - 1), ld(h, k))
                yp = jnp.where(lane_last, 0.0 if k == NK - 1 else lu(h, k + 1), lu(h, k))
                f = flow[z, pl.ds(h * S, S), pl.ds(k * L, L)]
                total = ((xm + xp) + (ym + yp)) + (at(z, h, k) + at(z + 2, h, k))
                new = keep * u(h, k) + KT * total
                new = new + s_x * jnp.where((f & 1) == 0, xm, xp)
                new = new + s_y * jnp.where(f < 2, ym, yp)
                put(z, h, k, new)

    def put_tin1(z, h, k, v):
        tin1[z + 1, k, pl.ds(S + h * S, S), :] = v

    def put_tin_o(z, h, k, v):
        tin_o[z, pl.ds(h * S, S), pl.ds(k * L, L)] = v

    def tin_range(src, put, first, last):
        def body(step, carry):
            for t in range(TU):
                tin_layer(src, put, step * TU + t)
            return carry

        lax.fori_loop(first, last, body, 0)

    def edge_flux(slot):
        for i in range(NI):
            at = pl.ds(i * S, S)

            def beside(s):
                return jnp.where(lane_even, pltpu.roll(cr[s, at, :], L - 1, 1), pltpu.roll(cl[s, at, :], 1, 1))

            if slot == 1:
                k = cs[0, at, :] + beside(0)
                kd[at, :] = jnp.where(lane_even, k, -k)
            fd[at, :] = kd[at, :] * (beside(slot) - cs[slot, at, :])

    def contact_flux(e, src):
        for j in range(NJ):
            for i in range(NI):
                at = pl.ds(i * S, S)
                pz[j, at, :] = HR * (src[0, j, pl.ds(S + i * S, S), :] - bb[e, j, at, :])

    def floor_layer(first, src, put, z):
        def at(ref, p, j, i, shift=0):
            return ref[p, j, pl.ds(S + i * S + shift, S), :]

        def face_x(j, i):
            if first:
                v = at(kh, z, j, i) + at(kh, z, j, i, 1)
                kx[z, j, pl.ds(S + i * S, S), :] = v
                return v
            return at(kx, z, j, i)

        def flux_x(j, i):
            return face_x(j, i) * (at(src, z, j, i, 1) - at(src, z, j, i))

        rx = [pltpu.roll(flux_x(j, -1), 1, 0) for j in range(NJ)]
        for i in range(NI):
            own = pl.ds(i * S, S)
            g = [at(src, z, j, i) for j in range(NJ)]
            edge = pltpu.roll(fd[own, :], L - 1 - 2 * z, 1)
            after = [pltpu.roll(v, L - 1, 1) for v in g]
            before = [pltpu.roll(v, 1, 1) for v in g]
            for j in range(NJ):
                if j == NJ - 1:
                    fy = jnp.where(lane_last, edge, kyp[z, j, own, :] * (after[j] - g[j]))
                else:
                    fy = kyp[z, j, own, :] * (jnp.where(lane_last, after[j + 1], after[j]) - g[j])
                if j == 0:
                    py = jnp.where(lane_first, edge, kym[z, j, own, :] * (g[j] - before[j]))
                else:
                    py = kym[z, j, own, :] * (g[j] - jnp.where(lane_first, before[j - 1], before[j]))
                fx = flux_x(j, i)
                rolled = pltpu.roll(fx, 1, 0)
                px = jnp.where(row_first, rx[j], rolled)
                rx[j] = rolled
                if first:
                    k_z = at(kh, z, j, i) + at(kh, z + 1, j, i)
                    kz[z, j, own, :] = k_z
                else:
                    k_z = kz[z, j, own, :]
                fz = k_z * (at(src, z + 1, j, i) - g[j])
                put(z, j, i, (g[j] + (fz - pz[j, own, :])) + ((fx - px) + (fy - py)))
                pz[j, own, :] = fz

    def pack_new(z):
        at = jnp.maximum(z, 0)
        for i in range(NI):
            own = pl.ds(S + i * S, S)
            pack_columns(2, z, i, floor1[at, 0, own, :], floor1[at, NJ - 1, own, :])

    def put_floor1(z, j, i, v):
        floor1[z, j, pl.ds(S + i * S, S), :] = v

    def put_floor_o(z, j, i, v):
        floor_o[z, pl.ds(i * S, S), pl.ds(j * L, L)] = v

    def floor_sweep(first, src, put):
        def body(step, carry):
            if first:
                for t in range(FU):
                    pack_new((step - 1) * FU + t)
            for t in range(FU):
                floor_layer(first, src, put, step * FU + t)
            return carry

        lax.fori_loop(0, ZF // FU, body, 0)
        if first:
            for t in range(FU):
                pack_new(ZF - FU + t)

    wait_recv_if(r0)

    def k_halo(z, carry):
        for j in range(NJ):
            for ok, at in ((rdn_ok, pl.ds(0, S)), (rup_ok, pl.ds(S + CX, S))):
                kh[z, j, at, :] = lookup(mat[z, j, at, :]) * ok.astype(jnp.float32)
        return carry

    lax.fori_loop(0, ZF, k_halo, 0, unroll=4)
    for m in b0:
        m.wait_recv()
    for m in own0:
        m.wait()
    contact_flux(0, floor0)
    wait_recv_if(c0)
    edge_flux(1)
    floor_sweep(True, floor0, put_floor1)
    start_if(r1)
    wait_send_if(c0)
    start_if(c1)
    for m in p1:
        m.start()
    own_p1.start()

    get_speeds.wait()
    for ld in get_tin:
        ld.wait()
    for m in p0:
        m.wait_recv()
    tin_ghosts(0, tin0)
    tin_copy_last(tin0)
    wait_recv_if(t0)

    def tin_part(q, carry):
        tin_range(tin0, put_tin1, q * (ZQ // TU), (q + 1) * (ZQ // TU))
        start_if(t1(q))

        @pl.when(q == 0)
        def _():
            for m in b1:
                m.start()
            own_b1.start()

        return carry

    lax.fori_loop(0, NQ, tin_part, 0)
    tin_copy_last(tin1)

    wait_recv_if(r1)
    wait_recv_if(c1)
    for m in b1:
        m.wait_recv()
    own_b1.wait()
    edge_flux(2)
    contact_flux(1, floor1)
    floor_sweep(False, floor1, put_floor_o)

    for m in p1:
        m.wait_recv()
    own_p1.wait()
    tin_ghosts(1, tin1)

    def tin_last(q, carry):
        wait_recv_if(t1(q))
        tin_range(tin1, put_tin_o, q * (ZQ // TU), (q + 1) * (ZQ // TU))
        return carry

    lax.fori_loop(0, NQ, tin_last, 0)

    for msgs in [t0, r0, r1, c1] + [t1(q) for q in range(NQ)]:
        wait_send_if(msgs)
    for m in p0 + b0 + p1 + b1:
        m.wait_send()


def local(n, ty, tin_temp, flow_code, speeds, floor_temp, material, conductivity):
    tin_shape = tin_temp.shape
    floor_shape = floor_temp.shape[1:]
    Z, R, NYW = tin_shape
    ZF, CX, CY = floor_shape
    NK, NJ = NYW // L, CY // L
    f32, i32 = jnp.float32, jnp.int32
    V = pltpu.VMEM
    tin_v, floor_v = V((Z + 2, NK, R + 2 * S, L), f32), V((ZF + 1, NJ, CX + 2 * S, L), f32)
    n_local = 4 + FQ * 2 * NJ + NK + 1 + 2 * NJ
    n_remote = 2 * NK + 4 * NJ + 6 + 2 * NQ + (2 * NJ + 2) * (ty - 1)
    tin_out, floor_out = pl.pallas_call(
        functools.partial(kernel, n, ty),
        out_shape=[V(tin_shape, f32), V(floor_shape, f32)],
        in_specs=[pl.BlockSpec(memory_space=pltpu.HBM)] * 6,
        out_specs=[pl.BlockSpec(memory_space=pltpu.VMEM)] * 2,
        scratch_shapes=[
            pltpu.SMEM(speeds.shape, f32), pltpu.SMEM(conductivity.shape, f32),
            tin_v, V(tin_shape, i32), tin_v, floor_v, V((ZF, NJ, CX + 2 * S, L), i32), floor_v,
            floor_v, V((ZF, NJ, CX + S, L), f32), V((ZF, NJ, CX, L), f32), V((ZF, NJ, CX, L), f32), V((ZF, NJ, CX, L), f32),
            V((NJ, CX, L), f32),
            V((3, CX, L), f32), V((3, CX, L), f32), V((3, CX, L), f32), V((CX, L), f32), V((CX, L), f32),
            V((2, NK, R, L), f32), V((2, NJ, CX, L), f32),
            pltpu.SemaphoreType.DMA((n_local,)),
            pltpu.SemaphoreType.DMA((n_remote,)),
            pltpu.SemaphoreType.DMA((n_remote,)),
        ],
        compiler_params=pltpu.CompilerParams(
            collective_id=0, has_side_effects=True, vmem_limit_bytes=52 * 1024 * 1024),
        cost_estimate=pl.CostEstimate(flops=120_000_000, bytes_accessed=23_000_000, transcendentals=0),
    )(tin_temp, flow_code, pltpu.with_memory_space_constraint(speeds, pltpu.HBM), floor_temp[0],
      material[0], pltpu.with_memory_space_constraint(conductivity, pltpu.HBM))
    return tin_out, floor_out[None]


def solution(mesh):
    n = mesh.shape["len"]
    split = ("grp", "len")
    placed = (P(None, split, None), P(None, split, None), P(),
              P(split, None, None, None), P(split, None, None, None), P())

    def whole(tin_temp, flow_code, speeds, floor_temp, material, conductivity):
        ty = tin_temp.shape[2] // floor_temp.shape[3]
        return jax.shard_map(
            functools.partial(local, n, ty),
            mesh=mesh,
            in_specs=placed,
            out_specs=(P(None, split, None), P(split, None, None, None)),
            check_vma=False,
        )(tin_temp, flow_code, speeds, floor_temp, material, conductivity)

    return whole
```

```python
import functools

import jax
import jax.numpy as jnp
from jax import lax
from jax.experimental import pallas as pl
from jax.experimental.pallas import tpu as pltpu
from jax.sharding import PartitionSpec as P

KT = 0.1
HT = 0.2
HR = 0.2
L = 128
S = 8
NQ = 2
FQ = 2
TU = 8
FU = 8
PU = 8
VA = 38
VB = 6


def floor_layer(kh, src, put, z, kx, kyp, kym, kz, pz, fd):
    NJ, NI = kyp.shape[1], kyp.shape[2] // S
    first = kh is not None
    lane = lax.broadcasted_iota(jnp.int32, (S, L), 1)
    lane_first, lane_last = lane == 0, lane == L - 1
    row_first = lax.broadcasted_iota(jnp.int32, (S, L), 0) == 0

    def at(ref, p, j, i, shift=0):
        return ref[p, j, pl.ds(S + i * S + shift, S), :]

    def face_x(j, i):
        if first:
            v = at(kh, z, j, i) + at(kh, z, j, i, 1)
            kx[z, j, pl.ds(S + i * S, S), :] = v
            return v
        return at(kx, z, j, i)

    def flux_x(j, i):
        return face_x(j, i) * (at(src, z, j, i, 1) - at(src, z, j, i))

    rx = [pltpu.roll(flux_x(j, -1), 1, 0) for j in range(NJ)]
    for i in range(NI):
        own = pl.ds(i * S, S)
        g = [at(src, z, j, i) for j in range(NJ)]
        edge = pltpu.roll(fd[own, :], L - 1 - 2 * z, 1)
        after = [pltpu.roll(v, L - 1, 1) for v in g]
        before = [pltpu.roll(v, 1, 1) for v in g]
        for j in range(NJ):
            if j == NJ - 1:
                fy = jnp.where(lane_last, edge, kyp[z, j, own, :] * (after[j] - g[j]))
            else:
                fy = kyp[z, j, own, :] * (jnp.where(lane_last, after[j + 1], after[j]) - g[j])
            if j == 0:
                py = jnp.where(lane_first, edge, kym[z, j, own, :] * (g[j] - before[j]))
            else:
                py = kym[z, j, own, :] * (g[j] - jnp.where(lane_first, before[j - 1], before[j]))
            fx = flux_x(j, i)
            rolled = pltpu.roll(fx, 1, 0)
            px = jnp.where(row_first, rx[j], rolled)
            rx[j] = rolled
            if first:
                k_z = at(kh, z, j, i) + at(kh, z + 1, j, i)
                kz[z, j, own, :] = k_z
            else:
                k_z = kz[z, j, own, :]
            fz = k_z * (at(src, z + 1, j, i) - g[j])
            put(z, j, i, (g[j] + (fz - pz[j, own, :])) + ((fx - px) + (fy - py)))
            pz[j, own, :] = fz


def kernel(n, ty, tin_h, flow_h, speeds_h, floor_h, mat_h, cond_h,
           tin_o, floor1, kx, kyp, kym, kz, pz, fd,
           speeds, cond, tin0, flow, tin1, floor0, mat, kh,
           cs, cl, cr, kd, pp, bb, load_sem, send_sem, recv_sem):
    Z, R, NYW = tin_h.shape
    ZF, CX, CY = floor_h.shape
    NH, NK = R // S, NYW // L
    NI, NJ = CX // S, CY // L
    ZQ, ZC = Z // NQ, ZF // FQ
    me = lax.axis_index("len")
    c = lax.rem(me, ty)
    base = me - c
    up_ok, dn_ok = me < n - 1, me > 0
    rup_ok, rdn_ok = me + ty < n, me >= ty
    cup_ok, cdn_ok = c < ty - 1, c > 0

    numbers = iter(range(10 ** 6))

    def local_copy(src, dst):
        return pltpu.make_async_copy(src, dst, load_sem.at[next(numbers)])

    get_cond, get_speeds = local_copy(cond_h, cond), local_copy(speeds_h, speeds)
    get_floor = []
    for q in range(FQ):
        part = pl.ds(q * ZC, ZC)
        get_floor.append(
            [local_copy(mat_h.at[part, :, pl.ds(j * L, L)], mat.at[part, j, pl.ds(S, CX), :]) for j in range(NJ)]
            + [local_copy(floor_h.at[part, :, pl.ds(j * L, L)], floor0.at[part, j, pl.ds(S, CX), :])
               for j in range(NJ)])
    get_tin = [local_copy(tin_h.at[:, :, pl.ds(k * L, L)], tin0.at[pl.ds(1, Z), k, pl.ds(S, R), :])
               for k in range(NK)] + [local_copy(flow_h, flow)]
    get_cond.start()
    get_speeds.start()

    barrier = pltpu.get_barrier_semaphore()

    def hello(target):
        pl.semaphore_signal(barrier, inc=1, device_id={"len": target},
                            device_id_type=pl.DeviceIdType.MESH)

    for d in range(1, ty):
        hello(base + lax.rem(c + d, ty))
    pairs = [(rup_ok, me + ty), (rdn_ok, me - ty),
             (jnp.logical_and(c == ty - 1, up_ok), me + 1),
             (jnp.logical_and(c == 0, dn_ok), me - 1)]
    for ok, target in pairs:
        @pl.when(ok)
        def _():
            hello(target)

    for group in get_floor:
        for ld in group:
            ld.start()

    row = lax.broadcasted_iota(jnp.int32, (S, L), 0)
    lane = lax.broadcasted_iota(jnp.int32, (S, L), 1)
    row_first = row == 0
    lane_first, lane_last = lane == 0, lane == L - 1
    lane_even = (lane & 1) == 0
    zero = jnp.zeros((S, L), jnp.float32)

    links = iter(range(10 ** 6))

    def remote(src, dst, target):
        e = next(links)
        return pltpu.make_async_remote_copy(
            src_ref=src, dst_ref=dst, send_sem=send_sem.at[e],
            recv_sem=recv_sem.at[e], device_id={"len": target},
            device_id_type=pl.DeviceIdType.MESH)

    def both_ways(up, down, ok_up, ok_dn):
        return [(ok_up, ok_dn, up), (ok_dn, ok_up, down)]

    lo, hi = S - 1, S + R
    flo, fhi = S - 1, S + CX
    layers = pl.ds(0, ZF)
    r0 = both_ways(
        [remote(a.at[:, CX - 1, pl.ds(j * L, L)], b.at[layers, j, flo, :], me + ty)
         for a, b in ((floor_h, floor0), (mat_h, mat)) for j in range(NJ)],
        [remote(a.at[:, 0, pl.ds(j * L, L)], b.at[layers, j, fhi, :], me - ty)
         for a, b in ((floor_h, floor0), (mat_h, mat)) for j in range(NJ)],
        rup_ok, rdn_ok)
    c0 = both_ways([remote(cs.at[0:2], cl.at[0:2], me + 1)], [remote(cs.at[0:2], cr.at[0:2], me - 1)],
                   cup_ok, cdn_ok)
    r1 = both_ways([remote(floor1.at[layers, :, S + CX - 1, :], floor1.at[layers, :, flo, :], me + ty)],
                   [remote(floor1.at[layers, :, S, :], floor1.at[layers, :, fhi, :], me - ty)],
                   rup_ok, rdn_ok)
    c1 = both_ways([remote(cs.at[2], cl.at[2], me + 1)], [remote(cs.at[2], cr.at[2], me - 1)],
                   cup_ok, cdn_ok)

    def p_into(e):
        return pp.at[e, pl.ds(NJ * c, NJ), :, :]

    def b_into(e):
        return bb.at[e, :, pl.ds(pl.multiple_of(c * R, S), R), :]

    def p_part(t):
        return floor1.at[0, :, pl.ds(pl.multiple_of(S + t * R, S), R), :]

    def b_part(t):
        return tin1.at[1, pl.ds(NJ * t, NJ), pl.ds(S, R), :]

    def p_parts(t):
        return [(floor_h.at[0, pl.ds(pl.multiple_of(t * R, S), R), pl.ds(j * L, L)], pp.at[0, NJ * c + j])
                for j in range(NJ)]

    def b_parts(t):
        return [(tin_h.at[0, :, pl.ds(pl.multiple_of((NJ * t + j) * L, L), L)],
                 bb.at[0, j, pl.ds(pl.multiple_of(c * R, S), R), :]) for j in range(NJ)]

    group = [lax.rem(c + d, ty) for d in range(1, ty)]
    p0 = [remote(*m, base + t) for t in group for m in p_parts(t)]
    b0 = [remote(*m, base + t) for t in group for m in b_parts(t)]
    p1 = [remote(p_part(t), p_into(1), base + t) for t in group]
    b1 = [remote(b_part(t), b_into(1), base + t) for t in group]
    own0 = [local_copy(*m) for m in p_parts(c) + b_parts(c)]
    own_p1, own_b1 = local_copy(p_part(c), p_into(1)), local_copy(b_part(c), b_into(1))
    t0_first, t1_first = next(links), next(links) + 2 * NQ - 1

    def tin_link(e, src, dst, target):
        return pltpu.make_async_remote_copy(
            src_ref=src, dst_ref=dst, send_sem=send_sem.at[e], recv_sem=recv_sem.at[e],
            device_id={"len": target}, device_id_type=pl.DeviceIdType.MESH)

    def t0_send(q):
        part, into = pl.ds(q * ZQ, ZQ), pl.ds(q * ZQ + 1, ZQ)
        e = t0_first + 2 * q
        for ok, way, src, dst, target in ((up_ok, 0, R - 1, lo, me + 1), (dn_ok, 1, 0, hi, me - 1)):
            @pl.when(ok)
            def _():
                for k in range(NK):
                    tin_link(e + way, tin_h.at[part, src, pl.ds(k * L, L)], tin0.at[into, k, dst, :], target).start()

    def t0(q):
        part = pl.ds(q * ZQ + 1, ZQ)
        e = t0_first + 2 * q
        return both_ways([tin_link(e, tin0.at[part, :, lo, :], tin0.at[part, :, lo, :], me + 1)],
                         [tin_link(e + 1, tin0.at[part, :, hi, :], tin0.at[part, :, hi, :], me - 1)], up_ok, dn_ok)

    def t1(q):
        part = pl.ds(q * ZQ + 1, ZQ)
        e = t1_first + 2 * q
        return both_ways(
            [tin_link(e, tin1.at[part, :, S + R - 1, :], tin1.at[part, :, lo, :], me + 1)],
            [tin_link(e + 1, tin1.at[part, :, S, :], tin1.at[part, :, hi, :], me - 1)], up_ok, dn_ok)

    def start_if(msgs):
        for ok, _, copies in msgs:
            @pl.when(ok)
            def _():
                for m in copies:
                    m.start()

    def wait_recv_if(msgs):
        for _, ok, copies in msgs:
            @pl.when(ok)
            def _():
                for m in copies:
                    m.wait_recv()

    def wait_send_if(msgs):
        for ok, _, copies in msgs:
            @pl.when(ok)
            def _():
                for m in copies:
                    m.wait_send()

    for m in own0:
        m.start()

    def clear(ok, fields, first):
        @pl.when(jnp.logical_not(ok))
        def _():
            for ref in fields:
                def body(z, carry):
                    for k in range(ref.shape[1]):
                        ref[z, k, pl.ds(first, S), :] = zero
                    return carry

                lax.fori_loop(0, ref.shape[0], body, 0)

    clear(dn_ok, (tin0, tin1), 0)
    clear(up_ok, (tin0, tin1), S + R)
    clear(rdn_ok, (floor0, floor1), 0)
    clear(rup_ok, (floor0, floor1), S + CX)
    for ok, ref in ((cdn_ok, cl), (cup_ok, cr)):
        @pl.when(jnp.logical_not(ok))
        def _():
            ref[...] = jnp.zeros_like(ref)
    cs[...] = jnp.zeros_like(cs)
    for ref in (floor0, floor1, kh):
        for j in range(NJ):
            for i in range(NI):
                ref[ZF, j, pl.ds(S + i * S, S), :] = zero

    peers = ty - 1
    for ok, _ in pairs:
        peers = peers + ok.astype(jnp.int32)
    pl.semaphore_wait(barrier, peers)
    start_if(r0)
    for m in b0 + p0:
        m.start()
    for q in range(NQ):
        t0_send(q)

    get_cond.wait()
    k0, k1, k2 = cond[0] * 0.5, cond[1] * 0.5, cond[2] * 0.5

    def lookup(m):
        return jnp.where(m == 0, k0, jnp.where(m == 1, k1, k2))

    def pack_columns(slot, z, i, first, last):
        mine = lax.shift_right_logical(lane, 1) == z
        both = pltpu.roll(jnp.where(lane_last, last, first), lax.rem(2 * z + 1 + L, L), 1)
        pltpu.store(cs.at[slot, pl.ds(i * S, S), :], both, mask=mine)

    def prepare(z, carry):
        for i in range(NI):
            at = pl.ds(S + i * S, S)
            k = [lookup(mat[z, j, at, :]) for j in range(NJ)]
            for j in range(NJ):
                kh[z, j, at, :] = k[j]
            pack_columns(0, z, i, k[0], k[NJ - 1])
            pack_columns(1, z, i, floor0[z, 0, at, :], floor0[z, NJ - 1, at, :])
        return carry

    def faces_y(z, carry):
        for i in range(NI):
            own = pl.ds(i * S, S)
            k = [kh[z, j, pl.ds(S + i * S, S), :] for j in range(NJ)]
            after = [pltpu.roll(v, L - 1, 1) for v in k]
            before = [pltpu.roll(v, 1, 1) for v in k]
            for j in range(NJ):
                kyp[z, j, own, :] = k[j] + (
                    after[j] if j == NJ - 1 else jnp.where(lane_last, after[j + 1], after[j]))
                kym[z, j, own, :] = k[j] + (
                    before[j] if j == 0 else jnp.where(lane_first, before[j - 1], before[j]))
        return carry

    for q in range(FQ):
        for ld in get_floor[q]:
            ld.wait()
        if q == FQ - 1:
            for ld in get_tin:
                ld.start()
        lax.fori_loop(q * ZC, (q + 1) * ZC, prepare, 0, unroll=PU)
    start_if(c0)
    lax.fori_loop(0, ZF, faces_y, 0, unroll=PU)

    def tin_ghosts(e, src):
        for k in range(NK):
            for h in range(NH):
                at = pl.ds(S + h * S, S)
                u = src[1, k, at, :]
                src[0, k, at, :] = u + (HT / KT) * (pp[e, k, pl.ds(h * S, S), :] - u)

    def tin_copy_last(src):
        for k in range(NK):
            src[Z + 1, k, pl.ds(S, R), :] = src[Z, k, pl.ds(S, R), :]

    def tin_layer(src, put, z):
        s_x, s_y = speeds[0, z], speeds[1, z]
        keep = (1.0 - 6.0 * KT) - s_x - s_y

        def at(p, h, k, shift=0):
            return src[p, k, pl.ds(S + h * S + shift, S), :]

        u = functools.cache(lambda h, k: at(z + 1, h, k))
        ld = functools.cache(lambda h, k: pltpu.roll(u(h, k), 1, 1))
        lu = functools.cache(lambda h, k: pltpu.roll(u(h, k), L - 1, 1))
        for k in range(NK):
            for h in range(NH):
                xm, xp = at(z + 1, h, k, -1), at(z + 1, h, k, 1)
                ym = jnp.where(lane_first, 0.0 if k == 0 else ld(h, k - 1), ld(h, k))
                yp = jnp.where(lane_last, 0.0 if k == NK - 1 else lu(h, k + 1), lu(h, k))
                f = flow[z, pl.ds(h * S, S), pl.ds(k * L, L)]
                total = ((xm + xp) + (ym + yp)) + (at(z, h, k) + at(z + 2, h, k))
                new = keep * u(h, k) + KT * total
                new = new + s_x * jnp.where((f & 1) == 0, xm, xp)
                new = new + s_y * jnp.where(f < 2, ym, yp)
                put(z, h, k, new)

    def put_tin1(z, h, k, v):
        tin1[z + 1, k, pl.ds(S + h * S, S), :] = v

    def put_tin_o(z, h, k, v):
        tin_o[z, pl.ds(h * S, S), pl.ds(k * L, L)] = v

    def tin_range(src, put, first, last):
        def body(step, carry):
            for t in range(TU):
                tin_layer(src, put, step * TU + t)
            return carry

        lax.fori_loop(first, last, body, 0)

    def edge_flux(slot):
        for i in range(NI):
            at = pl.ds(i * S, S)

            def beside(s):
                return jnp.where(lane_even, pltpu.roll(cr[s, at, :], L - 1, 1), pltpu.roll(cl[s, at, :], 1, 1))

            if slot == 1:
                k = cs[0, at, :] + beside(0)
                kd[at, :] = jnp.where(lane_even, k, -k)
            fd[at, :] = kd[at, :] * (beside(slot) - cs[slot, at, :])

    def contact_flux(e, src):
        for j in range(NJ):
            for i in range(NI):
                at = pl.ds(i * S, S)
                pz[j, at, :] = HR * (src[0, j, pl.ds(S + i * S, S), :] - bb[e, j, at, :])

    def pack_new(z):
        at = jnp.maximum(z, 0)
        for i in range(NI):
            own = pl.ds(S + i * S, S)
            pack_columns(2, z, i, floor1[at, 0, own, :], floor1[at, NJ - 1, own, :])

    def put_floor1(z, j, i, v):
        floor1[z, j, pl.ds(S + i * S, S), :] = v

    def floor_step(step, carry):
        for t in range(FU):
            pack_new((step - 1) * FU + t)
        for t in range(FU):
            floor_layer(kh, floor0, put_floor1, step * FU + t, kx, kyp, kym, kz, pz, fd)
        return carry

    get_speeds.wait()
    for ld in get_tin + own0:
        ld.wait()
    for m in p0:
        m.wait_recv()
    tin_ghosts(0, tin0)
    tin_copy_last(tin0)

    def tin_first_part(q, carry):
        wait_recv_if(t0(q))
        tin_range(tin0, put_tin1, q * (ZQ // TU), (q + 1) * (ZQ // TU))
        start_if(t1(q))

        @pl.when(q == 0)
        def _():
            for m in b1:
                m.start()
            own_b1.start()

        return carry

    lax.fori_loop(0, NQ, tin_first_part, 0)
    tin_copy_last(tin1)

    wait_recv_if(r0)

    def k_halo(z, carry):
        for j in range(NJ):
            for ok, at in ((rdn_ok, pl.ds(0, S)), (rup_ok, pl.ds(S + CX, S))):
                kh[z, j, at, :] = lookup(mat[z, j, at, :]) * ok.astype(jnp.float32)
        return carry

    lax.fori_loop(0, ZF, k_halo, 0, unroll=4)
    for m in b0:
        m.wait_recv()
    contact_flux(0, floor0)
    wait_recv_if(c0)
    edge_flux(1)
    lax.fori_loop(0, ZF // FU, floor_step, 0)
    for m in p1:
        m.start()
    own_p1.start()
    for t in range(FU):
        pack_new(ZF - FU + t)
    start_if(c1)
    start_if(r1)

    def tin_last(step, carry):
        q = lax.rem(step + 1, NQ)

        @pl.when(step == 0)
        def _():
            wait_recv_if(t1(0))

        @pl.when(step < NQ - 1)
        def _():
            wait_recv_if(t1(q))

        @pl.when(step == NQ - 1)
        def _():
            for m in p1:
                m.wait_recv()
            own_p1.wait()
            tin_ghosts(1, tin1)

        tin_range(tin1, put_tin_o, q * (ZQ // TU), (q + 1) * (ZQ // TU))
        return carry

    lax.fori_loop(0, NQ, tin_last, 0)

    for m in b1:
        m.wait_recv()
    own_b1.wait()
    contact_flux(1, floor1)
    wait_recv_if(c1)
    edge_flux(2)
    wait_recv_if(r1)

    for msgs in [c0, r0, r1, c1] + [t(q) for t in (t0, t1) for q in range(NQ)]:
        wait_send_if(msgs)
    for m in p0 + b0 + p1 + b1:
        m.wait_send()


def finish(tin_v, floor1, kx, kyp, kym, kz, pz_in, fd, tin_o, floor_o, floor_v, pz, sems):
    ZF, NJ, CX = kyp.shape[:3]
    out = pltpu.make_async_copy(tin_v, tin_o, sems.at[0])
    out.start()
    pz[...] = pz_in[...]

    def put(z, j, i, v):
        floor_v[z, pl.ds(i * S, S), pl.ds(j * L, L)] = v

    def part(step):
        rows = pl.ds(step * FU, FU)
        return pltpu.make_async_copy(floor_v.at[rows], floor_o.at[rows], sems.at[1 + step])

    def body(step, carry):
        for t in range(FU):
            floor_layer(None, floor1, put, step * FU + t, kx, kyp, kym, kz, pz, fd)
        part(step).start()
        return carry

    lax.fori_loop(0, ZF // FU, body, 0)
    for step in range(ZF // FU):
        part(step).wait()
    out.wait()


def local(n, ty, tin_temp, flow_code, speeds, floor_temp, material, conductivity):
    tin_shape = tin_temp.shape
    floor_shape = floor_temp.shape[1:]
    Z, R, NYW = tin_shape
    ZF, CX, CY = floor_shape
    NK, NJ = NYW // L, CY // L
    f32, i32 = jnp.float32, jnp.int32
    V = pltpu.VMEM
    tin_v, floor_v = V((Z + 2, NK, R + 2 * S, L), f32), V((ZF + 1, NJ, CX + 2 * S, L), f32)
    n_local = 4 + FQ * 2 * NJ + NK + 1 + 2 * NJ
    n_remote = 4 * NJ + 6 + 4 * NQ + (2 * NJ + 2) * (ty - 1)
    face = V((ZF, NJ, CX, L), f32)
    middle = pl.pallas_call(
        functools.partial(kernel, n, ty),
        out_shape=[V(tin_shape, f32), floor_v, V((ZF, NJ, CX + S, L), f32), face, face, face,
                   V((NJ, CX, L), f32), V((CX, L), f32)],
        in_specs=[pl.BlockSpec(memory_space=pltpu.HBM)] * 6,
        out_specs=[pl.BlockSpec(memory_space=pltpu.VMEM)] * 8,
        scratch_shapes=[
            pltpu.SMEM(speeds.shape, f32), pltpu.SMEM(conductivity.shape, f32),
            tin_v, V(tin_shape, i32), tin_v, floor_v, V((ZF, NJ, CX + 2 * S, L), i32), floor_v,
            V((3, CX, L), f32), V((3, CX, L), f32), V((3, CX, L), f32), V((CX, L), f32),
            V((2, NK, R, L), f32), V((2, NJ, CX, L), f32),
            pltpu.SemaphoreType.DMA((n_local,)),
            pltpu.SemaphoreType.DMA((n_remote,)),
            pltpu.SemaphoreType.DMA((n_remote,)),
        ],
        compiler_params=pltpu.CompilerParams(
            collective_id=0, has_side_effects=True, vmem_limit_bytes=VA * 1024 * 1024),
        cost_estimate=pl.CostEstimate(flops=120_000_000, bytes_accessed=23_000_000, transcendentals=0),
    )(tin_temp, flow_code, pltpu.with_memory_space_constraint(speeds, pltpu.HBM), floor_temp[0],
      material[0], pltpu.with_memory_space_constraint(conductivity, pltpu.HBM))
    tin_out, floor_out = pl.pallas_call(
        finish,
        out_shape=[jax.ShapeDtypeStruct(tin_shape, f32), jax.ShapeDtypeStruct(floor_shape, f32)],
        in_specs=[pl.BlockSpec(memory_space=pltpu.VMEM)] * 8,
        out_specs=[pl.BlockSpec(memory_space=pltpu.HBM)] * 2,
        scratch_shapes=[V(floor_shape, f32), V((NJ, CX, L), f32), pltpu.SemaphoreType.DMA((1 + ZF // FU,))],
        compiler_params=pltpu.CompilerParams(vmem_limit_bytes=VB * 1024 * 1024),
        cost_estimate=pl.CostEstimate(flops=20_000_000, bytes_accessed=8_000_000, transcendentals=0),
    )(*middle)
    return tin_out, floor_out[None]


def solution(mesh):
    n = mesh.shape["len"]
    split = ("grp", "len")
    placed = (P(None, split, None), P(None, split, None), P(),
              P(split, None, None, None), P(split, None, None, None), P())

    def whole(tin_temp, flow_code, speeds, floor_temp, material, conductivity):
        ty = tin_temp.shape[2] // floor_temp.shape[3]
        return jax.shard_map(
            functools.partial(local, n, ty),
            mesh=mesh,
            in_specs=placed,
            out_specs=(P(None, split, None), P(split, None, None, None)),
            check_vma=False,
        )(tin_temp, flow_code, speeds, floor_temp, material, conductivity)

    return whole
```

```python
import functools

import jax
import jax.numpy as jnp
from jax import lax
from jax.experimental import pallas as pl
from jax.experimental.pallas import tpu as pltpu
from jax.sharding import PartitionSpec as P

KT = 0.1
HT = 0.2
HR = 0.2
L = 128
S = 8
NQ = 2
FQ = 2
TU = 8
FU = 8
PU = 4
VA = 38
VB = 6


def floor_layer(kh, src, put, z, kx, kyp, kym, kz, pz, fd):
    NJ, NI = kyp.shape[1], kyp.shape[2] // S
    first = kh is not None
    lane = lax.broadcasted_iota(jnp.int32, (S, L), 1)
    lane_first, lane_last = lane == 0, lane == L - 1
    row_first = lax.broadcasted_iota(jnp.int32, (S, L), 0) == 0

    def at(ref, p, j, i, shift=0):
        return ref[p, j, pl.ds(S + i * S + shift, S), :]

    def face_x(j, i):
        if first:
            v = at(kh, z, j, i) + at(kh, z, j, i, 1)
            kx[z, j, pl.ds(S + i * S, S), :] = v
            return v
        return at(kx, z, j, i)

    def flux_x(j, i):
        return face_x(j, i) * (at(src, z, j, i, 1) - at(src, z, j, i))

    rx = [pltpu.roll(flux_x(j, -1), 1, 0) for j in range(NJ)]
    for i in range(NI):
        own = pl.ds(i * S, S)
        g = [at(src, z, j, i) for j in range(NJ)]
        edge = pltpu.roll(fd[own, :], L - 1 - 2 * z, 1)
        after = [pltpu.roll(v, L - 1, 1) for v in g]
        before = [pltpu.roll(v, 1, 1) for v in g]
        for j in range(NJ):
            if j == NJ - 1:
                fy = jnp.where(lane_last, edge, kyp[z, j, own, :] * (after[j] - g[j]))
            else:
                fy = kyp[z, j, own, :] * (jnp.where(lane_last, after[j + 1], after[j]) - g[j])
            if j == 0:
                py = jnp.where(lane_first, edge, kym[z, j, own, :] * (g[j] - before[j]))
            else:
                py = kym[z, j, own, :] * (g[j] - jnp.where(lane_first, before[j - 1], before[j]))
            fx = flux_x(j, i)
            rolled = pltpu.roll(fx, 1, 0)
            px = jnp.where(row_first, rx[j], rolled)
            rx[j] = rolled
            if first:
                k_z = at(kh, z, j, i) + at(kh, z + 1, j, i)
                kz[z, j, own, :] = k_z
            else:
                k_z = kz[z, j, own, :]
            fz = k_z * (at(src, z + 1, j, i) - g[j])
            put(z, j, i, (g[j] + (fz - pz[j, own, :])) + ((fx - px) + (fy - py)))
            pz[j, own, :] = fz


def kernel(n, ty, tin_h, flow_h, speeds_h, floor_h, mat_h, cond_h,
           tin_o, floor1, kx, kyp, kym, kz, pz, fd,
           speeds, cond, tin0, flow, tin1, floor0, mat, kh,
           cs, cl, cr, kd, pp, bb, load_sem, send_sem, recv_sem):
    Z, R, NYW = tin_h.shape
    ZF, CX, CY = floor_h.shape
    NH, NK = R // S, NYW // L
    NI, NJ = CX // S, CY // L
    ZQ, ZC = Z // NQ, ZF // FQ
    me = lax.axis_index("len")
    c = lax.rem(me, ty)
    base = me - c
    up_ok, dn_ok = me < n - 1, me > 0
    rup_ok, rdn_ok = me + ty < n, me >= ty
    cup_ok, cdn_ok = c < ty - 1, c > 0

    numbers = iter(range(10 ** 6))

    def local_copy(src, dst):
        return pltpu.make_async_copy(src, dst, load_sem.at[next(numbers)])

    get_cond, get_speeds = local_copy(cond_h, cond), local_copy(speeds_h, speeds)
    get_floor = []
    for q in range(FQ):
        part = pl.ds(q * ZC, ZC)
        get_floor.append(
            [local_copy(mat_h.at[part, :, pl.ds(j * L, L)], mat.at[part, j, pl.ds(S, CX), :]) for j in range(NJ)]
            + [local_copy(floor_h.at[part, :, pl.ds(j * L, L)], floor0.at[part, j, pl.ds(S, CX), :])
               for j in range(NJ)])
    get_tin = [local_copy(tin_h.at[:, :, pl.ds(k * L, L)], tin0.at[pl.ds(1, Z), k, pl.ds(S, R), :])
               for k in range(NK)] + [local_copy(flow_h, flow)]
    get_cond.start()
    get_speeds.start()

    barrier = pltpu.get_barrier_semaphore()

    def hello(target):
        pl.semaphore_signal(barrier, inc=1, device_id={"len": target},
                            device_id_type=pl.DeviceIdType.MESH)

    for d in range(1, ty):
        hello(base + lax.rem(c + d, ty))
    pairs = [(rup_ok, me + ty), (rdn_ok, me - ty),
             (jnp.logical_and(c == ty - 1, up_ok), me + 1),
             (jnp.logical_and(c == 0, dn_ok), me - 1)]
    for ok, target in pairs:
        @pl.when(ok)
        def _():
            hello(target)

    for group in get_floor:
        for ld in group:
            ld.start()

    row = lax.broadcasted_iota(jnp.int32, (S, L), 0)
    lane = lax.broadcasted_iota(jnp.int32, (S, L), 1)
    row_first = row == 0
    lane_first, lane_last = lane == 0, lane == L - 1
    lane_even = (lane & 1) == 0
    zero = jnp.zeros((S, L), jnp.float32)

    links = iter(range(10 ** 6))

    def remote(src, dst, target):
        e = next(links)
        return pltpu.make_async_remote_copy(
            src_ref=src, dst_ref=dst, send_sem=send_sem.at[e],
            recv_sem=recv_sem.at[e], device_id={"len": target},
            device_id_type=pl.DeviceIdType.MESH)

    def both_ways(up, down, ok_up, ok_dn):
        return [(ok_up, ok_dn, up), (ok_dn, ok_up, down)]

    lo, hi = S - 1, S + R
    flo, fhi = S - 1, S + CX
    layers = pl.ds(0, ZF)
    r0 = both_ways(
        [remote(a.at[:, CX - 1, pl.ds(j * L, L)], b.at[layers, j, flo, :], me + ty)
         for a, b in ((floor_h, floor0), (mat_h, mat)) for j in range(NJ)],
        [remote(a.at[:, 0, pl.ds(j * L, L)], b.at[layers, j, fhi, :], me - ty)
         for a, b in ((floor_h, floor0), (mat_h, mat)) for j in range(NJ)],
        rup_ok, rdn_ok)
    c0 = both_ways([remote(cs.at[0:2], cl.at[0:2], me + 1)], [remote(cs.at[0:2], cr.at[0:2], me - 1)],
                   cup_ok, cdn_ok)
    r1 = both_ways([remote(floor1.at[layers, :, S + CX - 1, :], floor1.at[layers, :, flo, :], me + ty)],
                   [remote(floor1.at[layers, :, S, :], floor1.at[layers, :, fhi, :], me - ty)],
                   rup_ok, rdn_ok)
    c1 = both_ways([remote(cs.at[2], cl.at[2], me + 1)], [remote(cs.at[2], cr.at[2], me - 1)],
                   cup_ok, cdn_ok)

    def p_into(e):
        return pp.at[e, pl.ds(NJ * c, NJ), :, :]

    def b_into(e):
        return bb.at[e, :, pl.ds(pl.multiple_of(c * R, S), R), :]

    def p_part(t):
        return floor1.at[0, :, pl.ds(pl.multiple_of(S + t * R, S), R), :]

    def b_part(t):
        return tin1.at[1, pl.ds(NJ * t, NJ), pl.ds(S, R), :]

    def p_parts(t):
        return [(floor_h.at[0, pl.ds(pl.multiple_of(t * R, S), R), pl.ds(j * L, L)], pp.at[0, NJ * c + j])
                for j in range(NJ)]

    def b_parts(t):
        return [(tin_h.at[0, :, pl.ds(pl.multiple_of((NJ * t + j) * L, L), L)],
                 bb.at[0, j, pl.ds(pl.multiple_of(c * R, S), R), :]) for j in range(NJ)]

    group = [lax.rem(c + d, ty) for d in range(1, ty)]
    p0 = [remote(*m, base + t) for t in group for m in p_parts(t)]
    b0 = [remote(*m, base + t) for t in group for m in b_parts(t)]
    p1 = [remote(p_part(t), p_into(1), base + t) for t in group]
    b1 = [remote(b_part(t), b_into(1), base + t) for t in group]
    own0 = [local_copy(*m) for m in p_parts(c) + b_parts(c)]
    own_p1, own_b1 = local_copy(p_part(c), p_into(1)), local_copy(b_part(c), b_into(1))
    t0_first, t1_first = next(links), next(links) + 2 * NQ - 1

    def tin_link(e, src, dst, target):
        return pltpu.make_async_remote_copy(
            src_ref=src, dst_ref=dst, send_sem=send_sem.at[e], recv_sem=recv_sem.at[e],
            device_id={"len": target}, device_id_type=pl.DeviceIdType.MESH)

    cross_up, cross_dn = jnp.logical_and(up_ok, c == ty - 1), jnp.logical_and(dn_ok, c == 0)

    def t0_send(q, oks):
        part, into = pl.ds(q * ZQ, ZQ), pl.ds(q * ZQ + 1, ZQ)
        e = t0_first + 2 * q
        for ok, way, src, dst, target in ((oks[0], 0, R - 1, lo, me + 1), (oks[1], 1, 0, hi, me - 1)):
            @pl.when(ok)
            def _():
                for k in range(NK):
                    tin_link(e + way, tin_h.at[part, src, pl.ds(k * L, L)], tin0.at[into, k, dst, :], target).start()

    def t0(q):
        part = pl.ds(q * ZQ + 1, ZQ)
        e = t0_first + 2 * q
        return both_ways([tin_link(e, tin0.at[part, :, lo, :], tin0.at[part, :, lo, :], me + 1)],
                         [tin_link(e + 1, tin0.at[part, :, hi, :], tin0.at[part, :, hi, :], me - 1)], up_ok, dn_ok)

    def t1(q):
        part = pl.ds(q * ZQ + 1, ZQ)
        e = t1_first + 2 * q
        return both_ways(
            [tin_link(e, tin1.at[part, :, S + R - 1, :], tin1.at[part, :, lo, :], me + 1)],
            [tin_link(e + 1, tin1.at[part, :, S, :], tin1.at[part, :, hi, :], me - 1)], up_ok, dn_ok)

    def start_if(msgs):
        for ok, _, copies in msgs:
            @pl.when(ok)
            def _():
                for m in copies:
                    m.start()

    def wait_recv_if(msgs):
        for _, ok, copies in msgs:
            @pl.when(ok)
            def _():
                for m in copies:
                    m.wait_recv()

    def wait_send_if(msgs):
        for ok, _, copies in msgs:
            @pl.when(ok)
            def _():
                for m in copies:
                    m.wait_send()

    for m in own0:
        m.start()

    def clear(ok, fields, first):
        @pl.when(jnp.logical_not(ok))
        def _():
            for ref in fields:
                def body(z, carry):
                    for k in range(ref.shape[1]):
                        ref[z, k, pl.ds(first, S), :] = zero
                    return carry

                lax.fori_loop(0, ref.shape[0], body, 0)

    clear(dn_ok, (tin0, tin1), 0)
    clear(up_ok, (tin0, tin1), S + R)
    clear(rdn_ok, (floor0, floor1), 0)
    clear(rup_ok, (floor0, floor1), S + CX)
    for ok, ref in ((cdn_ok, cl), (cup_ok, cr)):
        @pl.when(jnp.logical_not(ok))
        def _():
            ref[...] = jnp.zeros_like(ref)
    cs[...] = jnp.zeros_like(cs)
    for ref in (floor0, floor1, kh):
        for j in range(NJ):
            for i in range(NI):
                ref[ZF, j, pl.ds(S + i * S, S), :] = zero

    peers = ty - 1
    for ok, _ in pairs:
        peers = peers + ok.astype(jnp.int32)
    pl.semaphore_wait(barrier, peers)
    start_if(r0)
    for m in b0 + p0:
        m.start()
    t0_send(0, (up_ok, dn_ok))
    for q in range(1, NQ):
        t0_send(q, (cross_up, cross_dn))

    get_cond.wait()
    k0, k1, k2 = cond[0] * 0.5, cond[1] * 0.5, cond[2] * 0.5

    def lookup(m):
        return jnp.where(m == 0, k0, jnp.where(m == 1, k1, k2))

    def pack_columns(slot, z, i, first, last):
        mine = lax.shift_right_logical(lane, 1) == z
        both = pltpu.roll(jnp.where(lane_last, last, first), lax.rem(2 * z + 1 + L, L), 1)
        pltpu.store(cs.at[slot, pl.ds(i * S, S), :], both, mask=mine)

    def prepare(z, carry):
        for i in range(NI):
            at = pl.ds(S + i * S, S)
            k = [lookup(mat[z, j, at, :]) for j in range(NJ)]
            for j in range(NJ):
                kh[z, j, at, :] = k[j]
            pack_columns(0, z, i, k[0], k[NJ - 1])
            pack_columns(1, z, i, floor0[z, 0, at, :], floor0[z, NJ - 1, at, :])
        return carry

    def faces_y(z, carry):
        for i in range(NI):
            own = pl.ds(i * S, S)
            k = [kh[z, j, pl.ds(S + i * S, S), :] for j in range(NJ)]
            after = [pltpu.roll(v, L - 1, 1) for v in k]
            before = [pltpu.roll(v, 1, 1) for v in k]
            for j in range(NJ):
                kyp[z, j, own, :] = k[j] + (
                    after[j] if j == NJ - 1 else jnp.where(lane_last, after[j + 1], after[j]))
                kym[z, j, own, :] = k[j] + (
                    before[j] if j == 0 else jnp.where(lane_first, before[j - 1], before[j]))
        return carry

    for q in range(FQ):
        for ld in get_floor[q]:
            ld.wait()
        if q == FQ - 1:
            for ld in get_tin:
                ld.start()
        lax.fori_loop(q * ZC, (q + 1) * ZC, prepare, 0, unroll=PU)
    start_if(c0)
    for q in range(1, NQ):
        t0_send(q, (cup_ok, cdn_ok))
    lax.fori_loop(0, ZF, faces_y, 0, unroll=PU)

    def tin_ghosts(e, src):
        for k in range(NK):
            for h in range(NH):
                at = pl.ds(S + h * S, S)
                u = src[1, k, at, :]
                src[0, k, at, :] = u + (HT / KT) * (pp[e, k, pl.ds(h * S, S), :] - u)

    def tin_copy_last(src):
        for k in range(NK):
            src[Z + 1, k, pl.ds(S, R), :] = src[Z, k, pl.ds(S, R), :]

    def tin_layer(src, put, z):
        s_x, s_y = speeds[0, z], speeds[1, z]
        keep = (1.0 - 6.0 * KT) - s_x - s_y

        def at(p, h, k, shift=0):
            return src[p, k, pl.ds(S + h * S + shift, S), :]

        u = functools.cache(lambda h, k: at(z + 1, h, k))
        ld = functools.cache(lambda h, k: pltpu.roll(u(h, k), 1, 1))
        lu = functools.cache(lambda h, k: pltpu.roll(u(h, k), L - 1, 1))
        for k in range(NK):
            for h in range(NH):
                xm, xp = at(z + 1, h, k, -1), at(z + 1, h, k, 1)
                ym = jnp.where(lane_first, 0.0 if k == 0 else ld(h, k - 1), ld(h, k))
                yp = jnp.where(lane_last, 0.0 if k == NK - 1 else lu(h, k + 1), lu(h, k))
                f = flow[z, pl.ds(h * S, S), pl.ds(k * L, L)]
                total = ((xm + xp) + (ym + yp)) + (at(z, h, k) + at(z + 2, h, k))
                new = keep * u(h, k) + KT * total
                new = new + s_x * jnp.where((f & 1) == 0, xm, xp)
                new = new + s_y * jnp.where(f < 2, ym, yp)
                put(z, h, k, new)

    def put_tin1(z, h, k, v):
        tin1[z + 1, k, pl.ds(S + h * S, S), :] = v

    def put_tin_o(z, h, k, v):
        tin_o[z, pl.ds(h * S, S), pl.ds(k * L, L)] = v

    def tin_range(src, put, first, last):
        def body(step, carry):
            for t in range(TU):
                tin_layer(src, put, step * TU + t)
            return carry

        lax.fori_loop(first, last, body, 0)

    def edge_flux(slot):
        for i in range(NI):
            at = pl.ds(i * S, S)

            def beside(s):
                return jnp.where(lane_even, pltpu.roll(cr[s, at, :], L - 1, 1), pltpu.roll(cl[s, at, :], 1, 1))

            if slot == 1:
                k = cs[0, at, :] + beside(0)
                kd[at, :] = jnp.where(lane_even, k, -k)
            fd[at, :] = kd[at, :] * (beside(slot) - cs[slot, at, :])

    def contact_flux(e, src):
        for j in range(NJ):
            for i in range(NI):
                at = pl.ds(i * S, S)
                pz[j, at, :] = HR * (src[0, j, pl.ds(S + i * S, S), :] - bb[e, j, at, :])

    def pack_new(z):
        at = jnp.maximum(z, 0)
        for i in range(NI):
            own = pl.ds(S + i * S, S)
            pack_columns(2, z, i, floor1[at, 0, own, :], floor1[at, NJ - 1, own, :])

    def put_floor1(z, j, i, v):
        floor1[z, j, pl.ds(S + i * S, S), :] = v

    def floor_step(step, carry):
        for t in range(FU):
            pack_new((step - 1) * FU + t)
        for t in range(FU):
            floor_layer(kh, floor0, put_floor1, step * FU + t, kx, kyp, kym, kz, pz, fd)
        return carry

    get_speeds.wait()
    for ld in get_tin + own0:
        ld.wait()
    for m in p0:
        m.wait_recv()
    tin_ghosts(0, tin0)
    tin_copy_last(tin0)

    def k_halo(z, carry):
        for j in range(NJ):
            for ok, at in ((rdn_ok, pl.ds(0, S)), (rup_ok, pl.ds(S + CX, S))):
                kh[z, j, at, :] = lookup(mat[z, j, at, :]) * ok.astype(jnp.float32)
        return carry

    def first_sweep(q, carry):
        wait_recv_if(t0(q))
        tin_range(tin0, put_tin1, q * (ZQ // TU), (q + 1) * (ZQ // TU))
        start_if(t1(q))

        @pl.when(q == 0)
        def _():
            for m in b1:
                m.start()
            own_b1.start()
            wait_recv_if(r0)
            lax.fori_loop(0, ZF, k_halo, 0, unroll=4)
            for m in b0:
                m.wait_recv()
            contact_flux(0, floor0)
            wait_recv_if(c0)
            edge_flux(1)

        steps = ZF // FU // NQ
        lax.fori_loop(q * steps, (q + 1) * steps, floor_step, 0)

        @pl.when(q == 0)
        def _():
            for m in p1:
                m.start()
            own_p1.start()

        return carry

    lax.fori_loop(0, NQ, first_sweep, 0)
    tin_copy_last(tin1)
    for t in range(FU):
        pack_new(ZF - FU + t)
    start_if(c1)
    start_if(r1)

    for m in p1:
        m.wait_recv()
    own_p1.wait()
    tin_ghosts(1, tin1)

    def tin_last(q, carry):
        wait_recv_if(t1(q))
        tin_range(tin1, put_tin_o, q * (ZQ // TU), (q + 1) * (ZQ // TU))
        return carry

    lax.fori_loop(0, NQ, tin_last, 0)

    for m in b1:
        m.wait_recv()
    own_b1.wait()
    contact_flux(1, floor1)
    wait_recv_if(c1)
    edge_flux(2)
    wait_recv_if(r1)

    for msgs in [c0, r0, r1, c1] + [t(q) for t in (t0, t1) for q in range(NQ)]:
        wait_send_if(msgs)
    for m in p0 + b0 + p1 + b1:
        m.wait_send()


def finish(tin_v, floor1, kx, kyp, kym, kz, pz_in, fd, tin_o, floor_o, floor_v, pz, sems):
    ZF, NJ, CX = kyp.shape[:3]
    out = pltpu.make_async_copy(tin_v, tin_o, sems.at[0])
    out.start()
    pz[...] = pz_in[...]

    def put(z, j, i, v):
        floor_v[z, pl.ds(i * S, S), pl.ds(j * L, L)] = v

    def part(step):
        rows = pl.ds(step * FU, FU)
        return pltpu.make_async_copy(floor_v.at[rows], floor_o.at[rows], sems.at[1 + step])

    def body(step, carry):
        for t in range(FU):
            floor_layer(None, floor1, put, step * FU + t, kx, kyp, kym, kz, pz, fd)
        part(step).start()
        return carry

    lax.fori_loop(0, ZF // FU, body, 0)
    for step in range(ZF // FU):
        part(step).wait()
    out.wait()


def local(n, ty, tin_temp, flow_code, speeds, floor_temp, material, conductivity):
    tin_shape = tin_temp.shape
    floor_shape = floor_temp.shape[1:]
    Z, R, NYW = tin_shape
    ZF, CX, CY = floor_shape
    NK, NJ = NYW // L, CY // L
    f32, i32 = jnp.float32, jnp.int32
    V = pltpu.VMEM
    tin_v, floor_v = V((Z + 2, NK, R + 2 * S, L), f32), V((ZF + 1, NJ, CX + 2 * S, L), f32)
    n_local = 4 + FQ * 2 * NJ + NK + 1 + 2 * NJ
    n_remote = 4 * NJ + 6 + 4 * NQ + (2 * NJ + 2) * (ty - 1)
    face = V((ZF, NJ, CX, L), f32)
    middle = pl.pallas_call(
        functools.partial(kernel, n, ty),
        out_shape=[V(tin_shape, f32), floor_v, V((ZF, NJ, CX + S, L), f32), face, face, face,
                   V((NJ, CX, L), f32), V((CX, L), f32)],
        in_specs=[pl.BlockSpec(memory_space=pltpu.HBM)] * 6,
        out_specs=[pl.BlockSpec(memory_space=pltpu.VMEM)] * 8,
        scratch_shapes=[
            pltpu.SMEM(speeds.shape, f32), pltpu.SMEM(conductivity.shape, f32),
            tin_v, V(tin_shape, i32), tin_v, floor_v, V((ZF, NJ, CX + 2 * S, L), i32), floor_v,
            V((3, CX, L), f32), V((3, CX, L), f32), V((3, CX, L), f32), V((CX, L), f32),
            V((2, NK, R, L), f32), V((2, NJ, CX, L), f32),
            pltpu.SemaphoreType.DMA((n_local,)),
            pltpu.SemaphoreType.DMA((n_remote,)),
            pltpu.SemaphoreType.DMA((n_remote,)),
        ],
        compiler_params=pltpu.CompilerParams(
            collective_id=0, has_side_effects=True, vmem_limit_bytes=VA * 1024 * 1024),
        cost_estimate=pl.CostEstimate(flops=120_000_000, bytes_accessed=23_000_000, transcendentals=0),
    )(tin_temp, flow_code, pltpu.with_memory_space_constraint(speeds, pltpu.HBM), floor_temp[0],
      material[0], pltpu.with_memory_space_constraint(conductivity, pltpu.HBM))
    tin_out, floor_out = pl.pallas_call(
        finish,
        out_shape=[jax.ShapeDtypeStruct(tin_shape, f32), jax.ShapeDtypeStruct(floor_shape, f32)],
        in_specs=[pl.BlockSpec(memory_space=pltpu.VMEM)] * 8,
        out_specs=[pl.BlockSpec(memory_space=pltpu.HBM)] * 2,
        scratch_shapes=[V(floor_shape, f32), V((NJ, CX, L), f32), pltpu.SemaphoreType.DMA((1 + ZF // FU,))],
        compiler_params=pltpu.CompilerParams(vmem_limit_bytes=VB * 1024 * 1024),
        cost_estimate=pl.CostEstimate(flops=20_000_000, bytes_accessed=8_000_000, transcendentals=0),
    )(*middle)
    return tin_out, floor_out[None]


def solution(mesh):
    n = mesh.shape["len"]
    split = ("grp", "len")
    placed = (P(None, split, None), P(None, split, None), P(),
              P(split, None, None, None), P(split, None, None, None), P())

    def whole(tin_temp, flow_code, speeds, floor_temp, material, conductivity):
        ty = tin_temp.shape[2] // floor_temp.shape[3]
        return jax.shard_map(
            functools.partial(local, n, ty),
            mesh=mesh,
            in_specs=placed,
            out_specs=(P(None, split, None), P(split, None, None, None)),
            check_vma=False,
        )(tin_temp, flow_code, speeds, floor_temp, material, conductivity)

    return whole
```
